32 devices in a mesh: fsdp: 8 (over y, x, core), dp: 4 (over z).
Axes of the slice: x: 2, y: 2, z: 4, core: 2. Of those that a mesh axis runs over, the one named last changes fastest.
Arguments:
- teacher_hidden: bfloat16 [256, 8192], P(('fsdp', 'dp'))
- student_hidden: bfloat16 [256, 4096], P(('fsdp', 'dp'))
- teacher_head: bfloat16 [8192, 16384], P('dp', 'fsdp'), may hold values from -0.1875 to 0.1875
- student_head: bfloat16 [4096, 16384], P('dp', 'fsdp'), may hold values from -0.25 to 0.25
- actions: int32 [256], replicated, may hold values from 0 to 16383
- advantages: float32 [256], replicated, may hold values from -0.21875 to 0.21875
- loss_mask: int32 [256], replicated, may hold values 0 or 1
Outputs:
- token_loss: float32 [256], P('dp')
- head_grad: float32 [4096, 16384], P('dp', 'fsdp')
- hidden_grad: bfloat16 [256, 4096], P('fsdp', 'dp')
The draws below stay inside these ranges and needn't reach their ends.
All inputs are finite; a program needn't handle non-finite values.
Results may differ from the reference program's by a relative error of at most 0.0048.
Values may be sent and summed in bfloat16 or wider, within the bound.
A program may use at most 128 MiB of HBM per device.

```python
import jax
import jax.numpy as jnp

DT = 8192
DS = 4096
VOCAB = 16384
TOKENS = 256


def spread_rows(key, rows, cols):
    first, second = jax.random.split(key)
    values = jax.random.normal(first, (rows, cols), jnp.float32)
    scales = jnp.exp(jax.random.uniform(second, (rows,), jnp.float32, -1.3, -0.4))
    return values * scales[:, None]


def draw_teacher_hidden(key, part):
    return spread_rows(jax.random.fold_in(key, 11), TOKENS, DT).astype(jnp.bfloat16)


def draw_student_hidden(key, part):
    return spread_rows(jax.random.fold_in(key, 23), TOKENS, DS).astype(jnp.bfloat16)


def set_ends(array, stream_key, least, largest):
    place = [jax.random.randint(jax.random.fold_in(stream_key, axis), (), 0, length) for axis, length in enumerate(array.shape)]
    main_axis = array.shape.index(max(array.shape))
    neighbour = place[:main_axis] + [(place[main_axis] + 1) % array.shape[main_axis]] + place[main_axis + 1:]
    return array.at[tuple(place)].set(least).at[tuple(neighbour)].set(largest)


def block_levels(own_key, extent, shards, smallest, largest):
    def one(dim, shards_of):
        steps = jax.random.uniform(jax.random.fold_in(jax.random.fold_in(own_key, 6), dim), (shards_of,), jnp.float32, smallest / len(shards), largest / len(shards))
        return jnp.repeat(jnp.exp(steps), extent[dim] // shards_of).reshape((-1,) + (1,) * (len(extent) - dim - 1))

    loudness = one(*shards[0])
    for cut in shards[1:]:
        loudness = loudness * one(*cut)
    return loudness


def scatter_about(own_key, dims, scale, reach, shards=(), kind=jnp.bfloat16):
    gain = block_levels(own_key, dims, shards, -0.22, 0.18) if shards else 1.0
    array = jax.random.normal(own_key, dims, jnp.float32) * scale * gain
    return jnp.minimum(jnp.maximum(array, -reach), reach).astype(kind)


def setup_inputs(seed: int = 0) -> dict:
    arg_keys = jax.random.split(jax.random.key(seed), 8)
    teacher_hidden = draw_teacher_hidden(jax.random.fold_in(arg_keys[7], 71), 0)
    student_hidden = draw_student_hidden(jax.random.fold_in(arg_keys[7], 71), 0)
    teacher_head = scatter_about(arg_keys[2], (DT, VOCAB), (DT // 9) ** -0.5, 0.1875, ((0, 4), (1, 8)))
    student_head = scatter_about(arg_keys[3], (DS, VOCAB), (DS // 9) ** -0.5, 0.25, ((0, 4), (1, 8)))
    actions = set_ends(jax.random.randint(arg_keys[4], (TOKENS,), 0, VOCAB), jax.random.fold_in(arg_keys[4], 1), 0, VOCAB - 1).astype(jnp.int32)
    advantages = scatter_about(arg_keys[5], (TOKENS,), 0.015, 0.21875, (), jnp.float32)
    loss_mask = set_ends((jax.random.randint(arg_keys[6], (TOKENS,), 0, 4) < 3).astype(jnp.int32), jax.random.fold_in(arg_keys[6], 1), 0, 1)
    return dict(teacher_hidden=teacher_hidden, student_hidden=student_hidden, teacher_head=teacher_head, student_head=student_head, actions=actions, advantages=advantages, loss_mask=loss_mask)


kl_weight = 0.5


def reference(teacher_hidden, student_hidden, teacher_head, student_head, actions, advantages, loss_mask):
    teacher_logits = jnp.dot(teacher_hidden, teacher_head, preferred_element_type=jnp.float32)
    student_logits = jnp.dot(student_hidden, student_head, preferred_element_type=jnp.float32)
    teacher_max = jnp.max(teacher_logits, axis=1)
    student_max = jnp.max(student_logits, axis=1)
    teacher_exp = jnp.exp(teacher_logits - teacher_max[:, None])
    student_exp = jnp.exp(student_logits - student_max[:, None])
    teacher_sum = jnp.sum(teacher_exp, axis=1)
    student_sum = jnp.sum(student_exp, axis=1)
    teacher_lse = teacher_max + jnp.log(teacher_sum)
    student_lse = student_max + jnp.log(student_sum)
    teacher_prob = teacher_exp / teacher_sum[:, None]
    student_prob = student_exp / student_sum[:, None]
    kl = jnp.sum(teacher_prob * (teacher_logits - student_logits), axis=1) - teacher_lse + student_lse
    columns = jnp.arange(student_logits.shape[1], dtype=jnp.int32)
    onehot = (actions[:, None] == columns[None, :]).astype(jnp.float32)
    action_logp = jnp.sum(onehot * student_logits, axis=1) - student_lse
    weight = loss_mask.astype(jnp.float32)
    token_loss = weight * (kl_weight * kl - advantages * action_logp)
    logit_grad = (weight[:, None] * (kl_weight * (student_prob - teacher_prob) + advantages[:, None] * (student_prob - onehot))).astype(jnp.bfloat16)
    head_grad = jnp.dot(student_hidden.T, logit_grad, preferred_element_type=jnp.float32)
    hidden_grad = jnp.dot(logit_grad, student_head.T, preferred_element_type=jnp.float32).astype(jnp.bfloat16)
    return (token_loss, head_grad, hidden_grad)
```

```python
import functools

import jax
import jax.numpy as jnp
from jax import lax
from jax.experimental import pallas as pl
from jax.experimental.pallas import tpu as pltpu
from jax.sharding import PartitionSpec as P

KL_WEIGHT = 0.5
MESH = pl.DeviceIdType.MESH
PIECE = 32
LANES = 128
STEPS = 128.0
FULL = 32000.0
f32, bf16, i32, i16 = jnp.float32, jnp.bfloat16, jnp.int32, jnp.int16


def encode(x, out_ref):
    cols = x.shape[1]
    top = jnp.maximum(jnp.max(jnp.abs(x), axis=1, keepdims=True), 1e-30)
    code = jnp.floor(jnp.log2(top) * STEPS) + 2.0
    q = jnp.floor(x * (jnp.exp2(code * (-1.0 / STEPS)) * FULL) + 0.5)
    out_ref[:, :cols] = q.astype(i32).astype(i16)
    out_ref[:, cols:] = jnp.broadcast_to(code, (x.shape[0], LANES)).astype(i32).astype(i16)


def decode(in_ref, cols):
    code = in_ref[:, cols:].astype(i32).astype(f32)[:, 0:1]
    scale = jnp.exp2(code * (1.0 / STEPS)) * (1.0 / FULL)
    return in_ref[:, :cols].astype(i32).astype(f32) * scale


def main_kernel(
    F, D,
    th_ref, sh_ref, wt_hbm, ws_hbm, act_ref, adv_ref, mask_ref,
    loss_ref, hid_ref, rows_out, grad_out,
    wt, ws, zt, zs, gt, gs, rows_t, rows_s, part_t, part_s, line, xcol, stats, ycol, acol, lossbuf, grads, hg, pair_in, peer_in,
    w_sem, z_send, z_recv, ag_send, ag_recv, pr_send, pr_recv, l_send, l_recv, st_send, st_recv, g_send, g_recv,
    hp_send, hp_recv, hd_send, hd_recv, ls_send, ls_recv, out_sem,
):
    f, r = lax.axis_index("fsdp"), lax.axis_index("dp")
    T, V = part_t.shape
    J, H = F // 2, T // 2
    core, j = lax.rem(f, 2), f // 2
    partner = f + 1 - 2 * core
    upper = (r >= D // 2).astype(i32)
    step = 1 - 2 * upper
    end = jnp.minimum(r, D - 1 - r) == 0
    nblk = H // LANES
    NG = H // PIECE
    TB = T // F

    def remote(src, dst, ssem, rsem, **dev):
        return pltpu.make_async_remote_copy(
            src_ref=src, dst_ref=dst, send_sem=ssem, recv_sem=rsem, device_id=dev, device_id_type=MESH)

    w_s = pltpu.make_async_copy(ws_hbm, ws, w_sem.at[0])
    w_t = pltpu.make_async_copy(wt_hbm, wt, w_sem.at[1])
    w_s.start()
    w_t.start()

    barrier = pltpu.get_barrier_semaphore()
    for k in range(1, F):
        pl.semaphore_signal(barrier, inc=1, device_id={"fsdp": lax.rem(f + k, F)}, device_id_type=MESH)
    for k in range(1, D):
        pl.semaphore_signal(barrier, inc=1, device_id={"dp": lax.rem(r + k, D)}, device_id_type=MESH)

    hidden = ((sh_ref, zs, gs), (th_ref, zt, gt))
    for src, z, _ in hidden:
        x = src[...].astype(f32)
        half = z.shape[-1]
        for d in range(D):
            lo = x[:, 2 * d * half:(2 * d + 1) * half]
            hi = x[:, (2 * d + 1) * half:(2 * d + 2) * half]
            z[d] = jnp.concatenate([lo, hi], axis=0).astype(bf16)
    pl.semaphore_wait(barrier, F - 1 + D - 1)

    def z_copy(m, k):
        to = lax.rem(r + k, D)
        return remote(hidden[m][1].at[to], hidden[m][2].at[f, r], z_send.at[m, k], z_recv.at[m, k], dp=to)

    def z_in(m, k):
        return remote(hidden[m][1].at[0], hidden[m][2].at[f, lax.rem(r + D - k, D)], z_send.at[m, k], z_recv.at[m, k], dp=r)

    for m in range(2):
        for k in range(1, D):
            z_copy(m, k).start()
        hidden[m][2][f, r] = hidden[m][1][r]

    own = upper * H
    for b in range(nblk):
        a = act_ref[:, pl.ds(pl.multiple_of(own + b * LANES, LANES), LANES)].astype(f32)
        acol[b * LANES:(b + 1) * LANES, :] = jnp.broadcast_to(a, (LANES, LANES)).T

    def ag_copy(m, k):
        g = hidden[m][2]
        return remote(g.at[f], g.at[f], ag_send.at[m, k], ag_recv.at[m, k], fsdp=lax.rem(j + k, J) * 2 + core)

    def ag_slot(k):
        return lax.rem(j + J - k, J) * 2

    def pr_copy(m, k):
        g = hidden[m][2]
        s = ag_slot(k) + core
        return remote(g.at[s], g.at[s], pr_send.at[m, k], pr_recv.at[m, k], fsdp=partner)

    def pr_in(m, k):
        g = hidden[m][2]
        s = ag_slot(k) + 1 - core
        return remote(g.at[s], g.at[s], pr_send.at[m, k], pr_recv.at[m, k], fsdp=partner)

    for m in range(2):
        for k in range(1, D):
            z_in(m, k).wait_recv()
        for k in range(1, J):
            ag_copy(m, k).start()
        pr_copy(m, 0).start()

    def gather(m, rows):
        g = hidden[m][2]
        for k in range(1, J):
            s = ag_slot(k) + core
            remote(g.at[s], g.at[s], ag_send.at[m, k], ag_recv.at[m, k], fsdp=partner).wait_recv()
            pr_copy(m, k).start()
        for k in range(J):
            pr_in(m, k).wait_recv()
        half = g.shape[-1]
        n = g.shape[1] * 8

        @pl.loop(0, F)
        def _(b):
            x = g[b].astype(f32)
            at = pl.ds(pl.multiple_of(b * n, n), n)
            rows[at, :half] = x[:, 0:8, :].reshape(n, half).astype(bf16)
            rows[at, half:] = x[:, 8:16, :].reshape(n, half).astype(bf16)

    tile = min(512, V)

    def project(rows, w, part):
        @pl.loop(0, V // tile)
        def _(c):
            at = pl.ds(pl.multiple_of(c * tile, tile), tile)
            part[:, at] = jnp.dot(rows[...], w[:, at], preferred_element_type=f32)

    def line_copy(flow, i):
        to = jnp.clip(r + 1 - 2 * flow, 0, D - 1)
        return remote(line.at[flow, i], line.at[flow, i], l_send.at[flow, i], l_recv.at[flow, i], dp=to)

    near, far = upper, 1 - upper
    parts = (part_s, part_t)

    def own_rows(flow, i):
        return pl.ds(pl.multiple_of((1 - flow) * H + i * PIECE, PIECE), PIECE)

    def begin(m):
        @pl.when(end)
        def _():
            @pl.loop(0, NG)
            def _(i):
                encode(parts[m][own_rows(near, i), :], line.at[near, m * NG + i])
                line_copy(near, m * NG + i).start()

    def relay(m):
        @pl.when(jnp.logical_not(end))
        def _():
            @pl.loop(0, NG)
            def _(i):
                for flow in (near, far):
                    line_copy(flow, m * NG + i).wait_recv()
                    x = parts[m][own_rows(flow, i), :] + decode(line.at[flow, m * NG + i], V)
                    encode(x, line.at[flow, m * NG + i])
                    line_copy(flow, m * NG + i).start()

    def finish(m):
        @pl.loop(0, NG)
        def _(i):
            line_copy(far, m * NG + i).wait_recv()
            at = own_rows(far, i)
            parts[m][at, :] = parts[m][at, :] + decode(line.at[far, m * NG + i], V)

    gather(0, rows_s)
    w_s.wait()
    project(rows_s, ws, part_s)
    begin(0)
    rows_save = pltpu.make_async_copy(rows_s, rows_out, out_sem.at[0])
    rows_save.start()
    gather(1, rows_t)
    w_t.wait()
    project(rows_t, wt, part_t)
    begin(1)
    relay(0)
    relay(1)

    def st_copy(k):
        return remote(stats.at[f], stats.at[f], st_send.at[k], st_recv.at[k], fsdp=lax.rem(f + k, F))

    def st_in(k):
        s = lax.rem(f + F - k, F)
        return remote(stats.at[s], stats.at[s], st_send.at[k], st_recv.at[k], fsdp=s)

    def g_copy(half, i):
        at = pl.ds(pl.multiple_of(half * H + i * PIECE, PIECE), PIECE)
        to = jnp.clip(r + 1 - 2 * half, 0, D - 1)
        return remote(grads.at[at], grads.at[at], g_send.at[half, i], g_recv.at[half, i], dp=to)

    def loss_copy(k):
        return remote(lossbuf, lossbuf, ls_send.at[k], ls_recv.at[0], dp=r + step * k)

    lane = lax.broadcasted_iota(i32, (PIECE, LANES), 1)
    column = lax.broadcasted_iota(i32, (PIECE, V), 1) + f * V

    @pl.when(end)
    def _():
        finish(0)
        finish(1)

        @pl.loop(0, NG)
        def _(i):
            at = own_rows(far, i)
            here = pl.ds(pl.multiple_of(i * PIECE, PIECE), PIECE)
            lt, ls = part_t[at, :], part_s[at, :]
            mt, ms = jnp.max(lt, axis=1, keepdims=True), jnp.max(ls, axis=1, keepdims=True)
            et = jnp.exp(lt - mt)
            hit = column == acol[here, 0:1].astype(i32)
            values = (
                mt, ms, jnp.sum(et, axis=1, keepdims=True), jnp.sum(jnp.exp(ls - ms), axis=1, keepdims=True),
                jnp.sum(et * (lt - ls), axis=1, keepdims=True),
                jnp.sum(jnp.where(hit, ls, 0.0), axis=1, keepdims=True))
            x = jnp.zeros((PIECE, LANES), f32)
            for n, v in enumerate(values):
                x = jnp.where(lane == n, v, x)
            xcol[here, :] = x

        for b in range(nblk):
            stats[f, b * 8:(b + 1) * 8, :] = xcol[b * LANES:(b + 1) * LANES, :].T[0:8, :]
        for k in range(1, F):
            st_copy(k).start()
        for k in range(1, F):
            st_in(k).wait_recv()
        for b in range(nblk):
            s = stats[:, b * 8:(b + 1) * 8, :]
            mt, ms = s[:, 0:1, :], s[:, 1:2, :]
            top_t, top_s = jnp.max(mt, axis=0), jnp.max(ms, axis=0)
            scale_t = jnp.exp(mt - top_t[None])
            sum_t = jnp.sum(s[:, 2:3, :] * scale_t, axis=0)
            sum_s = jnp.sum(s[:, 3:4, :] * jnp.exp(ms - top_s[None]), axis=0)
            cross = jnp.sum(s[:, 4:5, :] * scale_t, axis=0)
            pick = jnp.sum(s[:, 5:6, :], axis=0)
            lse_t, lse_s = top_t + jnp.log(sum_t), top_s + jnp.log(sum_s)
            at = pl.ds(pl.multiple_of(own + b * LANES, LANES), LANES)
            weight, benefit = mask_ref[:, at].astype(f32), adv_ref[:, at]
            kl = cross / sum_t - lse_t + lse_s
            loss = weight * (KL_WEIGHT * kl - benefit * (pick - lse_s))
            lossbuf[b * 8:(b + 1) * 8, :] = jnp.broadcast_to(loss, (8, LANES))
            y = jnp.concatenate(
                [jnp.broadcast_to(v, (8, LANES)) for v in (lse_t, lse_s, weight, benefit)]
                + [jnp.zeros((LANES - 32, LANES), f32)], axis=0)
            ycol[b * LANES:(b + 1) * LANES, :] = y.T

        @pl.loop(0, NG)
        def _(i):
            at = own_rows(far, i)
            here = pl.ds(pl.multiple_of(i * PIECE, PIECE), PIECE)
            lse_t, lse_s = ycol[here, 0:1], ycol[here, 8:9]
            weight, benefit = ycol[here, 16:17], ycol[here, 24:25]
            tp, sp = jnp.exp(part_t[at, :] - lse_t), jnp.exp(part_s[at, :] - lse_s)
            hit = (column == acol[here, 0:1].astype(i32)).astype(f32)
            g = weight * (KL_WEIGHT * (sp - tp) + benefit * (sp - hit))
            grads[at, :] = g.astype(bf16)
            g_copy(upper, i).start()

        for k in range(1, D // 2):
            loss_copy(k).start()

    feature = ws.shape[0]
    ftile = min(256, feature)

    def back(half):
        at = pl.ds(pl.multiple_of(half * H, H), H)

        @pl.loop(0, feature // ftile)
        def _(c):
            cols = pl.ds(pl.multiple_of(c * ftile, ftile), ftile)
            y = lax.dot_general(grads[at, :], ws[cols, :], (((1,), (1,)), ((), ())), preferred_element_type=f32)
            hg[pl.ds(half * (J // 2), J // 2), :, :, cols] = y.reshape(J // 2, 2, TB, ftile)

    @pl.when(jnp.logical_not(end))
    def _():
        @pl.loop(0, NG)
        def _(i):
            g_copy(upper, i).wait_recv()
            g_copy(upper, i).start()
            g_copy(1 - upper, i).wait_recv()
            g_copy(1 - upper, i).start()
        back(upper)

    @pl.when(end)
    def _():
        back(upper)

        @pl.loop(0, NG)
        def _(i):
            g_copy(1 - upper, i).wait_recv()

    grad_save = pltpu.make_async_copy(grads, grad_out, out_sem.at[1])
    grad_save.start()
    back(1 - upper)

    pair = remote(hg.at[:, 1 - core], pair_in, hp_send, hp_recv, fsdp=partner)
    pair.start()
    pair.wait()

    @pl.loop(0, J)
    def _(b):
        hg[b, core] = hg[b, core] + pair_in[b]

    def hd_copy(k):
        to = lax.rem(j + k, J)
        return remote(hg.at[to, core], peer_in.at[j], hd_send.at[k], hd_recv.at[k], fsdp=to * 2 + core)

    def hd_in(k):
        s = lax.rem(j + J - k, J)
        return remote(hg.at[0, core], peer_in.at[s], hd_send.at[k], hd_recv.at[k], fsdp=f)

    for k in range(1, J):
        hd_copy(k).start()
    peer_in[j] = hg[j, core]

    @pl.when(jnp.logical_not(end))
    def _():
        loss_copy(0).wait_recv()
    for b in range(nblk):
        loss_ref[:, b * LANES:(b + 1) * LANES] = lossbuf[b * 8:b * 8 + 1, :]

    for k in range(1, J):
        hd_in(k).wait_recv()
    hid_ref[...] = jnp.sum(peer_in[...], axis=0).astype(bf16)

    for m in range(2):
        for k in range(1, D):
            z_copy(m, k).wait_send()
        for k in range(1, J):
            ag_copy(m, k).wait_send()
        for k in range(J):
            pr_copy(m, k).wait_send()
    for k in range(1, J):
        hd_copy(k).wait_send()

    @pl.loop(0, 2 * NG)
    def _(i):
        line_copy(near, i).wait_send()

    @pl.loop(0, NG)
    def _(i):
        g_copy(upper, i).wait_send()

    @pl.when(end)
    def _():
        for k in range(1, F):
            st_copy(k).wait_send()
        for k in range(1, D // 2):
            loss_copy(k).wait_send()

    @pl.when(jnp.logical_not(end))
    def _():
        @pl.loop(0, 2 * NG)
        def _(i):
            line_copy(far, i).wait_send()

        @pl.loop(0, NG)
        def _(i):
            g_copy(1 - upper, i).wait_send()

    rows_save.wait()
    grad_save.wait()


def head_grad_kernel(rows_ref, grad_ref, out_ref):
    out_ref[...] = lax.dot_general(
        rows_ref[...], grad_ref[...], (((0,), (0,)), ((), ())), preferred_element_type=f32)


def shards(F, D, teacher_hidden, student_hidden, teacher_head, student_head, actions, advantages, loss_mask):
    T = actions.shape[0]
    kt, V = teacher_head.shape
    ks = student_head.shape[0]
    mine = teacher_hidden.shape[0]
    J, H, TB = F // 2, T // 2, T // F
    NG, nblk = H // PIECE, H // LANES
    vmem = pl.BlockSpec(memory_space=pltpu.VMEM)
    hbm = pl.BlockSpec(memory_space=pl.ANY)
    dma = pltpu.SemaphoreType.DMA
    loss, hidden_grad, rows, grads = pl.pallas_call(
        functools.partial(main_kernel, F, D),
        out_shape=(
            jax.ShapeDtypeStruct((1, H), f32),
            jax.ShapeDtypeStruct((TB, ks), bf16),
            jax.ShapeDtypeStruct((T, ks), bf16),
            jax.ShapeDtypeStruct((T, V), bf16),
        ),
        in_specs=[vmem, vmem, hbm, hbm, vmem, vmem, vmem],
        out_specs=(vmem, vmem, hbm, hbm),
        scratch_shapes=[
            pltpu.VMEM((kt, V), bf16),
            pltpu.VMEM((ks, V), bf16),
            pltpu.VMEM((D, 2 * mine, kt // 2), bf16),
            pltpu.VMEM((D, 2 * mine, ks // 2), bf16),
            pltpu.VMEM((F, D, 2 * mine, kt // 2), bf16),
            pltpu.VMEM((F, D, 2 * mine, ks // 2), bf16),
            pltpu.VMEM((T, kt), bf16),
            pltpu.VMEM((T, ks), bf16),
            pltpu.VMEM((T, V), f32),
            pltpu.VMEM((T, V), f32),
            pltpu.VMEM((2, 2 * NG, PIECE, V + LANES), i16),
            pltpu.VMEM((H, LANES), f32),
            pltpu.VMEM((F, nblk * 8, LANES), f32),
            pltpu.VMEM((H, LANES), f32),
            pltpu.VMEM((H, LANES), f32),
            pltpu.VMEM((nblk * 8, LANES), f32),
            pltpu.VMEM((T, V), bf16),
            pltpu.VMEM((J, 2, TB, ks), f32),
            pltpu.VMEM((J, TB, ks), f32),
            pltpu.VMEM((J, TB, ks), f32),
            dma((2,)),
            dma((2, D)), dma((2, D)),
            dma((2, J)), dma((2, J)),
            dma((2, J)), dma((2, J)),
            dma((2, 2 * NG)), dma((2, 2 * NG)),
            dma((F,)), dma((F,)),
            dma((2, NG)), dma((2, NG)),
            dma, dma,
            dma((J,)), dma((J,)),
            dma((D,)), dma((1,)),
            dma((2,)),
        ],
        compiler_params=pltpu.CompilerParams(
            collective_id=0, has_side_effects=True, vmem_limit_bytes=63 * 2**20),
    )(teacher_hidden, student_hidden, teacher_head, student_head,
      actions.reshape(1, T), advantages.reshape(1, T), loss_mask.reshape(1, T))
    tile = min(256, V)
    head_grad = pl.pallas_call(
        head_grad_kernel,
        grid=(V // tile,),
        out_shape=jax.ShapeDtypeStruct((ks, V), f32),
        in_specs=[pl.BlockSpec((T, ks), lambda c: (0, 0)), pl.BlockSpec((T, tile), lambda c: (0, c))],
        out_specs=pl.BlockSpec((ks, tile), lambda c: (0, c)),
        compiler_params=pltpu.CompilerParams(vmem_limit_bytes=32 * 2**20),
    )(rows, grads)
    share = T // D
    first = lax.rem(lax.axis_index("dp"), D // 2) * share
    losses = lax.dynamic_slice_in_dim(loss.reshape(H), first, share)
    return losses, head_grad, hidden_grad


def solution(mesh):
    placed = (
        P(("fsdp", "dp"), None),
        P(("fsdp", "dp"), None),
        P("dp", "fsdp"),
        P("dp", "fsdp"),
        P(),
        P(),
        P(),
    )
    return jax.shard_map(
        functools.partial(shards, mesh.shape["fsdp"], mesh.shape["dp"]),
        mesh=mesh,
        in_specs=placed,
        out_specs=(P("dp"), P("dp", "fsdp"), P("fsdp", "dp")),
        check_vma=False,
    )
```

```python
import functools

import jax
import jax.numpy as jnp
from jax import lax
from jax.experimental import pallas as pl
from jax.experimental.pallas import tpu as pltpu
from jax.sharding import PartitionSpec as P

KL_WEIGHT = 0.5
MESH = pl.DeviceIdType.MESH
PIECE = 32
GPIECE = 16
LAG = 2
GLAG = 3
LANES = 128
STEPS = 128.0
FULL = 32000.0
f32, bf16, i32, i16 = jnp.float32, jnp.bfloat16, jnp.int32, jnp.int16


def encode(x, out_ref):
    cols = x.shape[1]
    top = jnp.maximum(jnp.max(jnp.abs(x), axis=1, keepdims=True), 1e-30)
    code = jnp.floor(jnp.log2(top) * STEPS) + 2.0
    q = jnp.floor(x * (jnp.exp2(code * (-1.0 / STEPS)) * FULL) + 0.5)
    out_ref[:, :cols] = q.astype(i32).astype(i16)
    out_ref[:, cols:] = jnp.broadcast_to(code, (x.shape[0], LANES)).astype(i32).astype(i16)


def decode(in_ref, cols):
    code = in_ref[:, cols:].astype(i32).astype(f32)[:, 0:1]
    scale = jnp.exp2(code * (1.0 / STEPS)) * (1.0 / FULL)
    return in_ref[:, :cols].astype(i32).astype(f32) * scale


def main_kernel(
    F, D,
    th_ref, sh_ref, wt_hbm, ws_hbm, act_ref, adv_ref, mask_ref,
    loss_ref, hid_ref, rows_out, grad_out,
    wt, ws, zt, zs, gt, gs, rows_t, rows_s, part, line, xcol, stats, ycol, acol, lossbuf, grads, hg, pair_in, peer_in,
    w_sem, z_send, z_recv, ag_send, ag_recv, pr_send, pr_recv, l_send, l_recv, st_send, st_recv, g_send, g_recv,
    hp_send, hp_recv, hd_send, hd_recv, ls_send, ls_recv, out_sem,
):
    f, r = lax.axis_index("fsdp"), lax.axis_index("dp")
    _, T, V = part.shape
    J, H = F // 2, T // 2
    core, j = lax.rem(f, 2), f // 2
    partner = f + 1 - 2 * core
    upper = (r >= D // 2).astype(i32)
    step = 1 - 2 * upper
    end = jnp.minimum(r, D - 1 - r) == 0
    nblk = H // LANES
    NG = H // PIECE
    GG = H // GPIECE
    TB = T // F

    def remote(src, dst, ssem, rsem, **dev):
        return pltpu.make_async_remote_copy(
            src_ref=src, dst_ref=dst, send_sem=ssem, recv_sem=rsem, device_id=dev, device_id_type=MESH)

    w_s = pltpu.make_async_copy(ws_hbm, ws, w_sem.at[0])
    w_t = pltpu.make_async_copy(wt_hbm, wt, w_sem.at[1])
    w_s.start()
    w_t.start()

    barrier = pltpu.get_barrier_semaphore()
    for k in range(1, F):
        pl.semaphore_signal(barrier, inc=1, device_id={"fsdp": lax.rem(f + k, F)}, device_id_type=MESH)
    for k in range(1, D):
        pl.semaphore_signal(barrier, inc=1, device_id={"dp": lax.rem(r + k, D)}, device_id_type=MESH)

    hidden = ((sh_ref, zs, gs), (th_ref, zt, gt))
    for src, z, _ in hidden:
        x = src[...].astype(f32)
        half = z.shape[-1]
        for d in range(D):
            lo = x[:, 2 * d * half:(2 * d + 1) * half]
            hi = x[:, (2 * d + 1) * half:(2 * d + 2) * half]
            z[d] = jnp.concatenate([lo, hi], axis=0).astype(bf16)
    pl.semaphore_wait(barrier, F - 1 + D - 1)

    def z_copy(m, k):
        to = lax.rem(r + k, D)
        return remote(hidden[m][1].at[to], hidden[m][2].at[f, r], z_send.at[m, k], z_recv.at[m, k], dp=to)

    def z_in(m, k):
        return remote(hidden[m][1].at[0], hidden[m][2].at[f, lax.rem(r + D - k, D)], z_send.at[m, k], z_recv.at[m, k], dp=r)

    for m in range(2):
        for k in range(1, D):
            z_copy(m, k).start()
        hidden[m][2][f, r] = hidden[m][1][r]

    own = upper * H
    for b in range(nblk):
        a = act_ref[:, pl.ds(pl.multiple_of(own + b * LANES, LANES), LANES)].astype(f32)
        acol[b * LANES:(b + 1) * LANES, :] = jnp.broadcast_to(a, (LANES, LANES)).T

    def ag_copy(m, k):
        g = hidden[m][2]
        return remote(g.at[f], g.at[f], ag_send.at[m, k], ag_recv.at[m, k], fsdp=lax.rem(j + k, J) * 2 + core)

    def ag_slot(k):
        return lax.rem(j + J - k, J) * 2

    def pr_copy(m, k):
        g = hidden[m][2]
        s = ag_slot(k) + core
        return remote(g.at[s], g.at[s], pr_send.at[m, k], pr_recv.at[m, k], fsdp=partner)

    def pr_in(m, k):
        g = hidden[m][2]
        s = ag_slot(k) + 1 - core
        return remote(g.at[s], g.at[s], pr_send.at[m, k], pr_recv.at[m, k], fsdp=partner)

    for m in range(2):
        for k in range(1, D):
            z_in(m, k).wait_recv()
        for k in range(1, J):
            ag_copy(m, k).start()
        pr_copy(m, 0).start()

    def gather(m, rows):
        g = hidden[m][2]
        for k in range(1, J):
            s = ag_slot(k) + core
            remote(g.at[s], g.at[s], ag_send.at[m, k], ag_recv.at[m, k], fsdp=partner).wait_recv()
            pr_copy(m, k).start()
        for k in range(J):
            pr_in(m, k).wait_recv()
        half = g.shape[-1]
        n = g.shape[1] * 8

        @pl.loop(0, F)
        def _(b):
            x = g[b].astype(f32)
            at = pl.ds(pl.multiple_of(b * n, n), n)
            rows[at, :half] = x[:, 0:8, :].reshape(n, half).astype(bf16)
            rows[at, half:] = x[:, 8:16, :].reshape(n, half).astype(bf16)

    tile = min(512, V)

    def project(rows, w, m):
        @pl.loop(0, V // tile)
        def _(c):
            at = pl.ds(pl.multiple_of(c * tile, tile), tile)
            part[m, :, at] = jnp.dot(rows[...], w[:, at], preferred_element_type=f32)

    def line_copy(flow, i):
        to = jnp.clip(r + 1 - 2 * flow, 0, D - 1)
        return remote(line.at[flow, i], line.at[flow, i], l_send.at[flow, i], l_recv.at[flow, i], dp=to)

    near, far = upper, 1 - upper

    def own_rows(flow, i):
        return pl.ds(pl.multiple_of((1 - flow) * H + i * PIECE, PIECE), PIECE)

    def begin(m):
        @pl.when(end)
        def _():
            @pl.loop(0, NG)
            def _(i):
                encode(part[m, own_rows(near, i), :], line.at[near, m * NG + i])
                line_copy(near, m * NG + i).start()

    def pass_on(flow, p):
        line_copy(flow, p).wait_recv()
        x = part[p // NG, own_rows(flow, lax.rem(p, NG)), :] + decode(line.at[flow, p], V)
        encode(x, line.at[flow, p])
        line_copy(flow, p).start()

    def relay(first, last):
        @pl.when(jnp.logical_not(end))
        def _():
            @pl.loop(first, last)
            def _(p):
                @pl.when(p < 2 * NG)
                def _():
                    pass_on(near, p)

                @pl.when(p >= LAG)
                def _():
                    pass_on(far, p - LAG)

    def finish(m, i):
        line_copy(far, m * NG + i).wait_recv()
        at = own_rows(far, i)
        x = part[m, at, :] + decode(line.at[far, m * NG + i], V)
        part[m, at, :] = x
        return x

    gather(0, rows_s)
    w_s.wait()
    project(rows_s, ws, 0)
    begin(0)
    rows_save = pltpu.make_async_copy(rows_s, rows_out, out_sem.at[0])
    rows_save.start()
    gather(1, rows_t)
    relay(0, NG // 2)
    w_t.wait()
    project(rows_t, wt, 1)
    begin(1)
    relay(NG // 2, 2 * NG + LAG)

    def st_copy(k):
        return remote(stats.at[f], stats.at[f], st_send.at[k], st_recv.at[k], fsdp=lax.rem(f + k, F))

    def st_in(k):
        s = lax.rem(f + F - k, F)
        return remote(stats.at[s], stats.at[s], st_send.at[k], st_recv.at[k], fsdp=s)

    def g_copy(half, i):
        at = pl.ds(pl.multiple_of(half * H + i * GPIECE, GPIECE), GPIECE)
        to = jnp.clip(r + 1 - 2 * half, 0, D - 1)
        return remote(grads.at[at], grads.at[at], g_send.at[half, i], g_recv.at[half, i], dp=to)

    def loss_copy(k):
        return remote(lossbuf, lossbuf, ls_send.at[k], ls_recv.at[0], dp=r + step * k)

    lane = lax.broadcasted_iota(i32, (PIECE, LANES), 1)
    column = lax.broadcasted_iota(i32, (PIECE, V), 1) + f * V

    @pl.when(end)
    def _():
        @pl.loop(0, NG)
        def _(i):
            finish(0, i)

        @pl.loop(0, NG)
        def _(i):
            here = pl.ds(pl.multiple_of(i * PIECE, PIECE), PIECE)
            lt = finish(1, i)
            ls = part[0, own_rows(far, i), :]
            mt, ms = jnp.max(lt, axis=1, keepdims=True), jnp.max(ls, axis=1, keepdims=True)
            et = jnp.exp(lt - mt)
            hit = column == acol[here, 0:1].astype(i32)
            values = (
                mt, ms, jnp.sum(et, axis=1, keepdims=True), jnp.sum(jnp.exp(ls - ms), axis=1, keepdims=True),
                jnp.sum(et * (lt - ls), axis=1, keepdims=True),
                jnp.sum(jnp.where(hit, ls, 0.0), axis=1, keepdims=True))
            x = jnp.zeros((PIECE, LANES), f32)
            for n, v in enumerate(values):
                x = jnp.where(lane == n, v, x)
            xcol[here, :] = x

        for b in range(nblk):
            stats[f, b * 8:(b + 1) * 8, :] = xcol[b * LANES:(b + 1) * LANES, :].T[0:8, :]
        for k in range(1, F):
            st_copy(k).start()
        for k in range(1, F):
            st_in(k).wait_recv()
        for b in range(nblk):
            s = stats[:, b * 8:(b + 1) * 8, :]
            mt, ms = s[:, 0:1, :], s[:, 1:2, :]
            top_t, top_s = jnp.max(mt, axis=0), jnp.max(ms, axis=0)
            scale_t = jnp.exp(mt - top_t[None])
            sum_t = jnp.sum(s[:, 2:3, :] * scale_t, axis=0)
            sum_s = jnp.sum(s[:, 3:4, :] * jnp.exp(ms - top_s[None]), axis=0)
            cross = jnp.sum(s[:, 4:5, :] * scale_t, axis=0)
            pick = jnp.sum(s[:, 5:6, :], axis=0)
            lse_t, lse_s = top_t + jnp.log(sum_t), top_s + jnp.log(sum_s)
            at = pl.ds(pl.multiple_of(own + b * LANES, LANES), LANES)
            weight, benefit = mask_ref[:, at].astype(f32), adv_ref[:, at]
            kl = cross / sum_t - lse_t + lse_s
            loss = weight * (KL_WEIGHT * kl - benefit * (pick - lse_s))
            lossbuf[b * 8:(b + 1) * 8, :] = jnp.broadcast_to(loss, (8, LANES))
            y = jnp.concatenate(
                [jnp.broadcast_to(v, (8, LANES)) for v in (lse_t, lse_s, weight, benefit)]
                + [jnp.zeros((LANES - 32, LANES), f32)], axis=0)
            ycol[b * LANES:(b + 1) * LANES, :] = y.T

        @pl.loop(0, NG)
        def _(i):
            at = own_rows(far, i)
            here = pl.ds(pl.multiple_of(i * PIECE, PIECE), PIECE)
            lse_t, lse_s = ycol[here, 0:1], ycol[here, 8:9]
            weight, benefit = ycol[here, 16:17], ycol[here, 24:25]
            tp, sp = jnp.exp(part[1, at, :] - lse_t), jnp.exp(part[0, at, :] - lse_s)
            hit = (column == acol[here, 0:1].astype(i32)).astype(f32)
            g = weight * (KL_WEIGHT * (sp - tp) + benefit * (sp - hit))
            grads[at, :] = g.astype(bf16)
            for n in range(PIECE // GPIECE):
                g_copy(upper, i * (PIECE // GPIECE) + n).start()

        for k in range(1, D // 2):
            loss_copy(k).start()

    feature = ws.shape[0]
    ftile = min(256, feature)

    def back(half):
        at = pl.ds(pl.multiple_of(half * H, H), H)

        @pl.loop(0, feature // ftile)
        def _(c):
            cols = pl.ds(pl.multiple_of(c * ftile, ftile), ftile)
            y = lax.dot_general(grads[at, :], ws[cols, :], (((1,), (1,)), ((), ())), preferred_element_type=f32)
            hg[pl.ds(half * (J // 2), J // 2), :, :, cols] = y.reshape(J // 2, 2, TB, ftile)

    def pair_copy(b):
        return remote(hg.at[b, 1 - core], pair_in.at[b], hp_send.at[b], hp_recv.at[b], fsdp=partner)

    def hd_copy(b):
        return remote(hg.at[b, core], peer_in.at[j], hd_send.at[b], hd_recv.at[j], fsdp=b * 2 + core)

    def hd_in(b):
        return remote(hg.at[b, core], peer_in.at[b], hd_send.at[b], hd_recv.at[b], fsdp=f)

    def pair_start(half):
        @pl.loop(0, J // 2)
        def _(n):
            pair_copy(half * (J // 2) + n).start()

    def share_out(half):
        @pl.loop(0, J // 2)
        def _(n):
            b = half * (J // 2) + n
            pair_copy(b).wait()
            y = hg[b, core] + pair_in[b]

            @pl.when(b == j)
            def _():
                peer_in[j] = y

            @pl.when(b != j)
            def _():
                hg[b, core] = y
                hd_copy(b).start()

    @pl.when(jnp.logical_not(end))
    def _():
        @pl.loop(0, GG + GLAG)
        def _(i):
            @pl.when(i < GG)
            def _():
                g_copy(upper, i).wait_recv()
                g_copy(upper, i).start()

            @pl.when(i >= GLAG)
            def _():
                g_copy(1 - upper, i - GLAG).wait_recv()
                g_copy(1 - upper, i - GLAG).start()

    back(upper)
    pair_start(upper)
    share_out(upper)

    @pl.when(end)
    def _():
        @pl.loop(0, GG)
        def _(i):
            g_copy(1 - upper, i).wait_recv()

    grad_save = pltpu.make_async_copy(grads, grad_out, out_sem.at[1])
    grad_save.start()
    back(1 - upper)
    pair_start(1 - upper)
    share_out(1 - upper)

    @pl.when(jnp.logical_not(end))
    def _():
        loss_copy(0).wait_recv()
    losses = jnp.concatenate([lossbuf[b * 8:b * 8 + 1, :] for b in range(nblk)], axis=1)
    share = T // D
    for q in range(D // 2):
        @pl.when(lax.rem(r, D // 2) == q)
        def _():
            loss_ref[...] = losses[:, q * share:(q + 1) * share]

    for k in range(1, J):
        hd_in(lax.rem(j + k, J)).wait_recv()
    hid_ref[...] = jnp.sum(peer_in[...], axis=0).astype(bf16)

    for m in range(2):
        for k in range(1, D):
            z_copy(m, k).wait_send()
        for k in range(1, J):
            ag_copy(m, k).wait_send()
        for k in range(J):
            pr_copy(m, k).wait_send()
    for k in range(1, J):
        hd_copy(lax.rem(j + k, J)).wait_send()

    @pl.loop(0, 2 * NG)
    def _(i):
        line_copy(near, i).wait_send()

    @pl.loop(0, GG)
    def _(i):
        g_copy(upper, i).wait_send()

    @pl.when(end)
    def _():
        for k in range(1, F):
            st_copy(k).wait_send()
        for k in range(1, D // 2):
            loss_copy(k).wait_send()

    @pl.when(jnp.logical_not(end))
    def _():
        @pl.loop(0, 2 * NG)
        def _(i):
            line_copy(far, i).wait_send()

        @pl.loop(0, GG)
        def _(i):
            g_copy(1 - upper, i).wait_send()

    rows_save.wait()
    grad_save.wait()


def head_grad_kernel(rows_ref, grad_ref, out_ref):
    out_ref[...] = lax.dot_general(
        rows_ref[...], grad_ref[...], (((0,), (0,)), ((), ())), preferred_element_type=f32)


def shards(F, D, teacher_hidden, student_hidden, teacher_head, student_head, actions, advantages, loss_mask):
    T = actions.shape[0]
    kt, V = teacher_head.shape
    ks = student_head.shape[0]
    mine = teacher_hidden.shape[0]
    J, H, TB = F // 2, T // 2, T // F
    NG, GG, nblk = H // PIECE, H // GPIECE, H // LANES
    vmem = pl.BlockSpec(memory_space=pltpu.VMEM)
    hbm = pl.BlockSpec(memory_space=pl.ANY)
    dma = pltpu.SemaphoreType.DMA
    loss, hidden_grad, rows, grads = pl.pallas_call(
        functools.partial(main_kernel, F, D),
        out_shape=(
            jax.ShapeDtypeStruct((1, T // D), f32),
            jax.ShapeDtypeStruct((TB, ks), bf16),
            jax.ShapeDtypeStruct((T, ks), bf16),
            jax.ShapeDtypeStruct((T, V), bf16),
        ),
        in_specs=[vmem, vmem, hbm, hbm, vmem, vmem, vmem],
        out_specs=(vmem, vmem, hbm, hbm),
        scratch_shapes=[
            pltpu.VMEM((kt, V), bf16),
            pltpu.VMEM((ks, V), bf16),
            pltpu.VMEM((D, 2 * mine, kt // 2), bf16),
            pltpu.VMEM((D, 2 * mine, ks // 2), bf16),
            pltpu.VMEM((F, D, 2 * mine, kt // 2), bf16),
            pltpu.VMEM((F, D, 2 * mine, ks // 2), bf16),
            pltpu.VMEM((T, kt), bf16),
            pltpu.VMEM((T, ks), bf16),
            pltpu.VMEM((2, T, V), f32),
            pltpu.VMEM((2, 2 * NG, PIECE, V + LANES), i16),
            pltpu.VMEM((H, LANES), f32),
            pltpu.VMEM((F, nblk * 8, LANES), f32),
            pltpu.VMEM((H, LANES), f32),
            pltpu.VMEM((H, LANES), f32),
            pltpu.VMEM((nblk * 8, LANES), f32),
            pltpu.VMEM((T, V), bf16),
            pltpu.VMEM((J, 2, TB, ks), f32),
            pltpu.VMEM((J, TB, ks), f32),
            pltpu.VMEM((J, TB, ks), f32),
            dma((2,)),
            dma((2, D)), dma((2, D)),
            dma((2, J)), dma((2, J)),
            dma((2, J)), dma((2, J)),
            dma((2, 2 * NG)), dma((2, 2 * NG)),
            dma((F,)), dma((F,)),
            dma((2, GG)), dma((2, GG)),
            dma((J,)), dma((J,)),
            dma((J,)), dma((J,)),
            dma((D,)), dma((1,)),
            dma((2,)),
        ],
        compiler_params=pltpu.CompilerParams(
            collective_id=0, has_side_effects=True, vmem_limit_bytes=63 * 2**20),
    )(teacher_hidden, student_hidden, teacher_head, student_head,
      actions.reshape(1, T), advantages.reshape(1, T), loss_mask.reshape(1, T))
    tile = min(256, V)
    head_grad = pl.pallas_call(
        head_grad_kernel,
        grid=(V // tile,),
        out_shape=jax.ShapeDtypeStruct((ks, V), f32),
        in_specs=[pl.BlockSpec((T, ks), lambda c: (0, 0)), pl.BlockSpec((T, tile), lambda c: (0, c))],
        out_specs=pl.BlockSpec((ks, tile), lambda c: (0, c)),
        compiler_params=pltpu.CompilerParams(vmem_limit_bytes=63 * 2**20),
    )(rows, grads)
    return loss.reshape(T // D), head_grad, hidden_grad


def solution(mesh):
    placed = (
        P(("fsdp", "dp"), None),
        P(("fsdp", "dp"), None),
        P("dp", "fsdp"),
        P("dp", "fsdp"),
        P(),
        P(),
        P(),
    )
    return jax.shard_map(
        functools.partial(shards, mesh.shape["fsdp"], mesh.shape["dp"]),
        mesh=mesh,
        in_specs=placed,
        out_specs=(P("dp"), P("dp", "fsdp"), P("fsdp", "dp")),
        check_vma=False,
    )
```

```python
import functools

import jax
import jax.numpy as jnp
from jax import lax
from jax.experimental import pallas as pl
from jax.experimental.pallas import tpu as pltpu
from jax.sharding import PartitionSpec as P

KL_WEIGHT = 0.5
MESH = pl.DeviceIdType.MESH
PIECE = 32
GPIECE = 16
LAG = 2
GLAG = 3
CHUNK = 64
LANES = 128
STEPS = 128.0
FULL = 32000.0
f32, bf16, i32, i16 = jnp.float32, jnp.bfloat16, jnp.int32, jnp.int16


def encode(x, out_ref):
    cols = x.shape[1]
    top = jnp.maximum(jnp.max(jnp.abs(x), axis=1, keepdims=True), 1e-30)
    code = jnp.floor(jnp.log2(top) * STEPS) + 2.0
    q = jnp.floor(x * (jnp.exp2(code * (-1.0 / STEPS)) * FULL) + 0.5)
    out_ref[:, :cols] = q.astype(i32).astype(i16)
    out_ref[:, cols:] = jnp.broadcast_to(code, (x.shape[0], LANES)).astype(i32).astype(i16)


def decode(in_ref, cols):
    code = in_ref[:, cols:].astype(i32).astype(f32)[:, 0:1]
    scale = jnp.exp2(code * (1.0 / STEPS)) * (1.0 / FULL)
    return in_ref[:, :cols].astype(i32).astype(f32) * scale


def main_kernel(
    F, D,
    th_ref, sh_ref, wt_hbm, ws_hbm, act_ref, adv_ref, mask_ref,
    loss_ref, hid_ref, rows_out, grad_out,
    wt, ws, zt, zs, gt, gs, rows_t, rows_s, part, line, xcol, stats, ycol, acol, lossbuf, grads, pair_in, peer_in,
    w_sem, z_send, z_recv, ag_send, ag_recv, pr_send, pr_recv, l_send, l_recv, st_send, st_recv, g_send, g_recv,
    hp_send, hp_recv, hd_send, hd_recv, ls_send, ls_recv, out_sem,
):
    f, r = lax.axis_index("fsdp"), lax.axis_index("dp")
    _, T, V = part.shape
    J, H = F // 2, T // 2
    core, j = lax.rem(f, 2), f // 2
    partner = f + 1 - 2 * core
    upper = (r >= D // 2).astype(i32)
    step = 1 - 2 * upper
    end = jnp.minimum(r, D - 1 - r) == 0
    nblk, NC = H // LANES, H // CHUNK
    NG = H // PIECE
    GG = H // GPIECE
    TB = T // F

    def remote(src, dst, ssem, rsem, **dev):
        return pltpu.make_async_remote_copy(
            src_ref=src, dst_ref=dst, send_sem=ssem, recv_sem=rsem, device_id=dev, device_id_type=MESH)

    w_s = pltpu.make_async_copy(ws_hbm, ws, w_sem.at[0])
    w_t = pltpu.make_async_copy(wt_hbm, wt, w_sem.at[1])
    w_s.start()
    w_t.start()

    barrier = pltpu.get_barrier_semaphore()
    for k in range(1, F):
        pl.semaphore_signal(barrier, inc=1, device_id={"fsdp": lax.rem(f + k, F)}, device_id_type=MESH)
    for k in range(1, D):
        pl.semaphore_signal(barrier, inc=1, device_id={"dp": lax.rem(r + k, D)}, device_id_type=MESH)

    hidden = ((sh_ref, zs, gs), (th_ref, zt, gt))
    for src, z, _ in hidden:
        x = src[...].astype(f32)
        half = z.shape[-1]
        for d in range(D):
            lo = x[:, 2 * d * half:(2 * d + 1) * half]
            hi = x[:, (2 * d + 1) * half:(2 * d + 2) * half]
            z[d] = jnp.concatenate([lo, hi], axis=0).astype(bf16)
    pl.semaphore_wait(barrier, F - 1 + D - 1)

    def z_copy(m, k):
        to = lax.rem(r + k, D)
        return remote(hidden[m][1].at[to], hidden[m][2].at[f, r], z_send.at[m, k], z_recv.at[m, k], dp=to)

    def z_in(m, k):
        return remote(hidden[m][1].at[0], hidden[m][2].at[f, lax.rem(r + D - k, D)], z_send.at[m, k], z_recv.at[m, k], dp=r)

    for m in range(2):
        for k in range(1, D):
            z_copy(m, k).start()
        hidden[m][2][f, r] = hidden[m][1][r]

    own = upper * H
    for b in range(nblk):
        a = act_ref[:, pl.ds(pl.multiple_of(own + b * LANES, LANES), LANES)].astype(f32)
        acol[b * LANES:(b + 1) * LANES, :] = jnp.broadcast_to(a, (LANES, LANES)).T

    def ag_copy(m, k):
        g = hidden[m][2]
        return remote(g.at[f], g.at[f], ag_send.at[m, k], ag_recv.at[m, k], fsdp=lax.rem(j + k, J) * 2 + core)

    def ag_slot(k):
        return lax.rem(j + J - k, J) * 2

    def pr_copy(m, k):
        g = hidden[m][2]
        s = ag_slot(k) + core
        return remote(g.at[s], g.at[s], pr_send.at[m, k], pr_recv.at[m, k], fsdp=partner)

    def pr_in(m, k):
        g = hidden[m][2]
        s = ag_slot(k) + 1 - core
        return remote(g.at[s], g.at[s], pr_send.at[m, k], pr_recv.at[m, k], fsdp=partner)

    for m in range(2):
        for k in range(1, D):
            z_in(m, k).wait_recv()
        for k in range(1, J):
            ag_copy(m, k).start()
        pr_copy(m, 0).start()

    def gather(m, rows):
        g = hidden[m][2]
        for k in range(1, J):
            s = ag_slot(k) + core
            remote(g.at[s], g.at[s], ag_send.at[m, k], ag_recv.at[m, k], fsdp=partner).wait_recv()
            pr_copy(m, k).start()
        for k in range(J):
            pr_in(m, k).wait_recv()
        half = g.shape[-1]
        n = g.shape[1] * 8

        @pl.loop(0, F)
        def _(b):
            x = g[b].astype(f32)
            at = pl.ds(pl.multiple_of(b * n, n), n)
            rows[at, :half] = x[:, 0:8, :].reshape(n, half).astype(bf16)
            rows[at, half:] = x[:, 8:16, :].reshape(n, half).astype(bf16)

    tile = max(LANES, min(V, 2**17 // T))

    def project(rows, w, m):
        @pl.loop(0, V // tile)
        def _(c):
            at = pl.ds(pl.multiple_of(c * tile, tile), tile)
            part[m, :, at] = jnp.dot(rows[...], w[:, at], preferred_element_type=f32)

    def line_copy(flow, i):
        to = jnp.clip(r + 1 - 2 * flow, 0, D - 1)
        return remote(line.at[flow, i], line.at[flow, i], l_send.at[flow, i], l_recv.at[flow, i], dp=to)

    near, far = upper, 1 - upper

    def own_rows(flow, i):
        return pl.ds(pl.multiple_of((1 - flow) * H + i * PIECE, PIECE), PIECE)

    def begin(m):
        @pl.when(end)
        def _():
            @pl.loop(0, NG)
            def _(i):
                encode(part[m, own_rows(near, i), :], line.at[near, m * NG + i])
                line_copy(near, m * NG + i).start()

    def pass_on(flow, p):
        line_copy(flow, p).wait_recv()
        x = part[p // NG, own_rows(flow, lax.rem(p, NG)), :] + decode(line.at[flow, p], V)
        encode(x, line.at[flow, p])
        line_copy(flow, p).start()

    def relay(first, last):
        @pl.when(jnp.logical_not(end))
        def _():
            @pl.loop(first, last)
            def _(p):
                @pl.when(p < 2 * NG)
                def _():
                    pass_on(near, p)

                @pl.when(p >= LAG)
                def _():
                    pass_on(far, p - LAG)

    def finish(m, i):
        line_copy(far, m * NG + i).wait_recv()
        at = own_rows(far, i)
        x = part[m, at, :] + decode(line.at[far, m * NG + i], V)
        part[m, at, :] = x
        return x

    gather(0, rows_s)
    w_s.wait()
    project(rows_s, ws, 0)
    begin(0)
    gather(1, rows_t)
    relay(0, NG // 2)
    w_t.wait()
    project(rows_t, wt, 1)
    begin(1)
    relay(NG // 2, 2 * NG + LAG)

    rows_x = wt.at[:ws.shape[0], :T]

    @pl.loop(0, T // LANES)
    def _(b):
        at = pl.ds(pl.multiple_of(b * LANES, LANES), LANES)
        rows_x[:, at] = rows_s[at, :].astype(f32).T.astype(bf16)

    rows_save = pltpu.make_async_copy(rows_x, rows_out, out_sem.at[0])
    rows_save.start()

    def st_copy(c, k):
        return remote(stats.at[c, f], stats.at[c, f], st_send.at[c, k], st_recv.at[c, k], fsdp=lax.rem(f + k, F))

    def st_in(c, k):
        s = lax.rem(f + F - k, F)
        return remote(stats.at[c, s], stats.at[c, s], st_send.at[c, k], st_recv.at[c, k], fsdp=s)

    def g_copy(half, i):
        at = pl.ds(pl.multiple_of(half * H + i * GPIECE, GPIECE), GPIECE)
        to = jnp.clip(r + 1 - 2 * half, 0, D - 1)
        return remote(grads.at[at], grads.at[at], g_send.at[half, i], g_recv.at[half, i], dp=to)

    def loss_copy(k):
        return remote(lossbuf, lossbuf, ls_send.at[k], ls_recv.at[0], dp=r + step * k)

    lane = lax.broadcasted_iota(i32, (PIECE, LANES), 1)
    column = lax.broadcasted_iota(i32, (PIECE, V), 1) + f * V

    @pl.when(end)
    def _():
        xcol[...] = jnp.zeros_like(xcol)

        @pl.loop(0, NG)
        def _(i):
            finish(0, i)

        def finish_chunk(c):
            block = pl.ds(c * CHUNK // LANES * LANES, LANES)
            first, last = c * CHUNK // PIECE, (c + 1) * CHUNK // PIECE

            @pl.loop(first, last)
            def _(i):
                here = pl.ds(pl.multiple_of(i * PIECE, PIECE), PIECE)
                lt = finish(1, i)
                ls = part[0, own_rows(far, i), :]
                mt, ms = jnp.max(lt, axis=1, keepdims=True), jnp.max(ls, axis=1, keepdims=True)
                et = jnp.exp(lt - mt)
                hit = column == acol[here, 0:1].astype(i32)
                values = (
                    mt, ms, jnp.sum(et, axis=1, keepdims=True), jnp.sum(jnp.exp(ls - ms), axis=1, keepdims=True),
                    jnp.sum(et * (lt - ls), axis=1, keepdims=True),
                    jnp.sum(jnp.where(hit, ls, 0.0), axis=1, keepdims=True))
                x = jnp.zeros((PIECE, LANES), f32)
                for n, v in enumerate(values):
                    x = jnp.where(lane == n, v, x)
                xcol[here, :] = x

            stats[c, f] = xcol[block, :].T[0:8, :]
            for k in range(1, F):
                st_copy(c, k).start()
            for k in range(1, F):
                st_in(c, k).wait_recv()
            s = stats[c]
            mt, ms = s[:, 0:1, :], s[:, 1:2, :]
            top_t, top_s = jnp.max(mt, axis=0), jnp.max(ms, axis=0)
            scale_t = jnp.exp(mt - top_t[None])
            sum_t = jnp.sum(s[:, 2:3, :] * scale_t, axis=0)
            sum_s = jnp.sum(s[:, 3:4, :] * jnp.exp(ms - top_s[None]), axis=0)
            cross = jnp.sum(s[:, 4:5, :] * scale_t, axis=0)
            pick = jnp.sum(s[:, 5:6, :], axis=0)
            lse_t, lse_s = top_t + jnp.log(sum_t), top_s + jnp.log(sum_s)
            at = pl.ds(pl.multiple_of(own + c * CHUNK // LANES * LANES, LANES), LANES)
            weight, benefit = mask_ref[:, at].astype(f32), adv_ref[:, at]
            kl = cross / sum_t - lse_t + lse_s
            loss = weight * (KL_WEIGHT * kl - benefit * (pick - lse_s))
            lossbuf[c * 8:(c + 1) * 8, :] = jnp.broadcast_to(loss, (8, LANES))
            y = jnp.concatenate(
                [jnp.broadcast_to(v, (8, LANES)) for v in (lse_t, lse_s, weight, benefit)]
                + [jnp.zeros((LANES - 32, LANES), f32)], axis=0)
            skip = c * CHUNK % LANES
            ycol[c * CHUNK:(c + 1) * CHUNK, :] = y.T[skip:skip + CHUNK, :]

            @pl.loop(first, last)
            def _(i):
                at = own_rows(far, i)
                here = pl.ds(pl.multiple_of(i * PIECE, PIECE), PIECE)
                lse_t, lse_s = ycol[here, 0:1], ycol[here, 8:9]
                weight, benefit = ycol[here, 16:17], ycol[here, 24:25]
                tp, sp = jnp.exp(part[1, at, :] - lse_t), jnp.exp(part[0, at, :] - lse_s)
                hit = (column == acol[here, 0:1].astype(i32)).astype(f32)
                g = weight * (KL_WEIGHT * (sp - tp) + benefit * (sp - hit))
                grads[at, :] = g.astype(bf16)
                for n in range(PIECE // GPIECE):
                    g_copy(upper, i * (PIECE // GPIECE) + n).start()

        for c in range(NC):
            finish_chunk(c)

        for k in range(1, D // 2):
            loss_copy(k).start()

    feature = ws.shape[0]
    ftile = min(256, feature)

    def back(half):
        at = pl.ds(pl.multiple_of(half * H, H), H)

        @pl.loop(0, feature // ftile)
        def _(c):
            cols = pl.ds(pl.multiple_of(c * ftile, ftile), ftile)
            y = lax.dot_general(grads[at, :], ws[cols, :], (((1,), (1,)), ((), ())), preferred_element_type=f32)
            part[0, at, cols] = y

    def hg(b, c):
        at = pl.ds(pl.multiple_of((b * 2 + c) * TB, TB), TB)
        return part.at[0, at, :feature]

    def pair_copy(b):
        return remote(hg(b, 1 - core), pair_in.at[b], hp_send.at[b], hp_recv.at[b], fsdp=partner)

    def hd_copy(b):
        return remote(hg(b, core), peer_in.at[j], hd_send.at[b], hd_recv.at[j], fsdp=b * 2 + core)

    def hd_in(b):
        return remote(hg(b, core), peer_in.at[b], hd_send.at[b], hd_recv.at[b], fsdp=f)

    def pair_start(half):
        @pl.loop(0, J // 2)
        def _(n):
            pair_copy(half * (J // 2) + n).start()

    def share_out(half):
        @pl.loop(0, J // 2)
        def _(n):
            b = half * (J // 2) + n
            pair_copy(b).wait()
            y = hg(b, core)[...] + pair_in[b]

            @pl.when(b == j)
            def _():
                peer_in[j] = y

            @pl.when(b != j)
            def _():
                hg(b, core)[...] = y
                hd_copy(b).start()

    @pl.when(jnp.logical_not(end))
    def _():
        @pl.loop(0, GG + GLAG)
        def _(i):
            @pl.when(i < GG)
            def _():
                g_copy(upper, i).wait_recv()
                g_copy(upper, i).start()

            @pl.when(i >= GLAG)
            def _():
                g_copy(1 - upper, i - GLAG).wait_recv()
                g_copy(1 - upper, i - GLAG).start()

    back(upper)
    pair_start(upper)
    share_out(upper)

    @pl.when(end)
    def _():
        @pl.loop(0, GG)
        def _(i):
            g_copy(1 - upper, i).wait_recv()

    grad_save = pltpu.make_async_copy(grads, grad_out, out_sem.at[1])
    grad_save.start()
    back(1 - upper)
    pair_start(1 - upper)
    share_out(1 - upper)

    @pl.when(jnp.logical_not(end))
    def _():
        loss_copy(0).wait_recv()
    losses = jnp.concatenate(
        [lossbuf[c * 8:c * 8 + 1, c * CHUNK % LANES:c * CHUNK % LANES + CHUNK] for c in range(NC)], axis=1)
    share = T // D
    for q in range(D // 2):
        @pl.when(lax.rem(r, D // 2) == q)
        def _():
            loss_ref[...] = losses[:, q * share:(q + 1) * share]

    for k in range(1, J):
        hd_in(lax.rem(j + k, J)).wait_recv()
    hid_ref[...] = jnp.sum(peer_in[...], axis=0).astype(bf16)

    for m in range(2):
        for k in range(1, D):
            z_copy(m, k).wait_send()
        for k in range(1, J):
            ag_copy(m, k).wait_send()
        for k in range(J):
            pr_copy(m, k).wait_send()
    for k in range(1, J):
        hd_copy(lax.rem(j + k, J)).wait_send()

    @pl.loop(0, 2 * NG)
    def _(i):
        line_copy(near, i).wait_send()

    @pl.loop(0, GG)
    def _(i):
        g_copy(upper, i).wait_send()

    @pl.when(end)
    def _():
        for k in range(1, F):
            for c in range(NC):
                st_copy(c, k).wait_send()
        for k in range(1, D // 2):
            loss_copy(k).wait_send()

    @pl.when(jnp.logical_not(end))
    def _():
        @pl.loop(0, 2 * NG)
        def _(i):
            line_copy(far, i).wait_send()

        @pl.loop(0, GG)
        def _(i):
            g_copy(1 - upper, i).wait_send()

    rows_save.wait()
    grad_save.wait()


def head_grad_kernel(rows_ref, grad_ref, out_ref):
    out_ref[...] = jnp.dot(rows_ref[...], grad_ref[...], preferred_element_type=f32)


def shards(F, D, teacher_hidden, student_hidden, teacher_head, student_head, actions, advantages, loss_mask):
    T = actions.shape[0]
    kt, V = teacher_head.shape
    ks = student_head.shape[0]
    mine = teacher_hidden.shape[0]
    J, H, TB = F // 2, T // 2, T // F
    NG, GG, NC = H // PIECE, H // GPIECE, H // CHUNK
    vmem = pl.BlockSpec(memory_space=pltpu.VMEM)
    hbm = pl.BlockSpec(memory_space=pl.ANY)
    dma = pltpu.SemaphoreType.DMA
    loss, hidden_grad, rows, grads = pl.pallas_call(
        functools.partial(main_kernel, F, D),
        out_shape=(
            jax.ShapeDtypeStruct((1, T // D), f32),
            jax.ShapeDtypeStruct((TB, ks), bf16),
            jax.ShapeDtypeStruct((ks, T), bf16),
            jax.ShapeDtypeStruct((T, V), bf16),
        ),
        in_specs=[vmem, vmem, hbm, hbm, vmem, vmem, vmem],
        out_specs=(vmem, vmem, hbm, hbm),
        scratch_shapes=[
            pltpu.VMEM((kt, V), bf16),
            pltpu.VMEM((ks, V), bf16),
            pltpu.VMEM((D, 2 * mine, kt // 2), bf16),
            pltpu.VMEM((D, 2 * mine, ks // 2), bf16),
            pltpu.VMEM((F, D, 2 * mine, kt // 2), bf16),
            pltpu.VMEM((F, D, 2 * mine, ks // 2), bf16),
            pltpu.VMEM((T, kt), bf16),
            pltpu.VMEM((T, ks), bf16),
            pltpu.VMEM((2, T, V), f32),
            pltpu.VMEM((2, 2 * NG, PIECE, V + LANES), i16),
            pltpu.VMEM((H, LANES), f32),
            pltpu.VMEM((NC, F, 8, LANES), f32),
            pltpu.VMEM((H, LANES), f32),
            pltpu.VMEM((H, LANES), f32),
            pltpu.VMEM((NC * 8, LANES), f32),
            pltpu.VMEM((T, V), bf16),
            pltpu.VMEM((J, TB, ks), f32),
            pltpu.VMEM((J, TB, ks), f32),
            dma((2,)),
            dma((2, D)), dma((2, D)),
            dma((2, J)), dma((2, J)),
            dma((2, J)), dma((2, J)),
            dma((2, 2 * NG)), dma((2, 2 * NG)),
            dma((NC, F)), dma((NC, F)),
            dma((2, GG)), dma((2, GG)),
            dma((J,)), dma((J,)),
            dma((J,)), dma((J,)),
            dma((D,)), dma((1,)),
            dma((2,)),
        ],
        compiler_params=pltpu.CompilerParams(
            collective_id=0, has_side_effects=True, vmem_limit_bytes=63 * 2**20),
    )(teacher_hidden, student_hidden, teacher_head, student_head,
      actions.reshape(1, T), advantages.reshape(1, T), loss_mask.reshape(1, T))
    tile = min(256, V)
    head_grad = pl.pallas_call(
        head_grad_kernel,
        grid=(V // tile,),
        out_shape=jax.ShapeDtypeStruct((ks, V), f32),
        in_specs=[pl.BlockSpec((ks, T), lambda c: (0, 0)), pl.BlockSpec((T, tile), lambda c: (0, c))],
        out_specs=pl.BlockSpec((ks, tile), lambda c: (0, c)),
        compiler_params=pltpu.CompilerParams(vmem_limit_bytes=63 * 2**20),
    )(rows, grads)
    return loss.reshape(T // D), head_grad, hidden_grad


def solution(mesh):
    placed = (
        P(("fsdp", "dp"), None),
        P(("fsdp", "dp"), None),
        P("dp", "fsdp"),
        P("dp", "fsdp"),
        P(),
        P(),
        P(),
    )
    return jax.shard_map(
        functools.partial(shards, mesh.shape["fsdp"], mesh.shape["dp"]),
        mesh=mesh,
        in_specs=placed,
        out_specs=(P("dp"), P("dp", "fsdp"), P("fsdp", "dp")),
        check_vma=False,
    )
```

```python
import functools

import jax
import jax.numpy as jnp
from jax import lax
from jax.experimental import pallas as pl
from jax.experimental.pallas import tpu as pltpu
from jax.sharding import PartitionSpec as P

KL_WEIGHT = 0.5
MESH = pl.DeviceIdType.MESH
PIECE = 16
GPIECE = 16
LAG = 4
GLAG = 3
CHUNK = 64
LANES = 128
STEPS = 128.0
FULL = 32000.0
MIDDLE = 32768
f32, bf16, i32, i16 = jnp.float32, jnp.bfloat16, jnp.int32, jnp.int16


def encode(x, out_ref):
    cols = x.shape[1]
    top = jnp.maximum(jnp.max(jnp.abs(x), axis=1, keepdims=True), 1e-30)
    code = jnp.floor(jnp.log2(top) * STEPS) + 2.0
    q = x * (jnp.exp2(code * (-1.0 / STEPS)) * FULL) + (MIDDLE + 0.5)
    out_ref[:, :cols] = (q.astype(i32) - MIDDLE).astype(i16)
    out_ref[:, cols:] = jnp.broadcast_to(code, (x.shape[0], LANES)).astype(i32).astype(i16)


def decode(in_ref, cols):
    code = in_ref[:, cols:].astype(i32).astype(f32)[:, 0:1]
    scale = jnp.exp2(code * (1.0 / STEPS)) * (1.0 / FULL)
    return in_ref[:, :cols].astype(i32).astype(f32) * scale


def main_kernel(
    F, D,
    th_ref, sh_ref, wt_hbm, ws_hbm, act_ref, adv_ref, mask_ref,
    loss_ref, hid_ref, rows_out, grad_out,
    wt, ws, zt, zs, gt, gs, rows_t, rows_s, part, line, xcol, stats, ycol, acol, lossbuf, grads, pair_in, peer_in,
    w_sem, z_send, z_recv, ag_send, ag_recv, pr_send, pr_recv, l_send, l_recv, st_send, st_recv, g_send, g_recv,
    hp_send, hp_recv, hd_send, hd_recv, ls_send, ls_recv, out_sem,
):
    f, r = lax.axis_index("fsdp"), lax.axis_index("dp")
    _, T, V = part.shape
    J, H = F // 2, T // 2
    core, j = lax.rem(f, 2), f // 2
    partner = f + 1 - 2 * core
    upper = (r >= D // 2).astype(i32)
    step = 1 - 2 * upper
    end = jnp.minimum(r, D - 1 - r) == 0
    nblk, NC = H // LANES, H // CHUNK
    NG = H // PIECE
    GG = H // GPIECE
    TB = T // F

    def remote(src, dst, ssem, rsem, **dev):
        return pltpu.make_async_remote_copy(
            src_ref=src, dst_ref=dst, send_sem=ssem, recv_sem=rsem, device_id=dev, device_id_type=MESH)

    w_s = pltpu.make_async_copy(ws_hbm, ws, w_sem.at[0])
    w_t = pltpu.make_async_copy(wt_hbm, wt, w_sem.at[1])
    w_s.start()
    w_t.start()

    barrier = pltpu.get_barrier_semaphore()
    for k in range(1, F):
        pl.semaphore_signal(barrier, inc=1, device_id={"fsdp": lax.rem(f + k, F)}, device_id_type=MESH)
    for k in range(1, D):
        pl.semaphore_signal(barrier, inc=1, device_id={"dp": lax.rem(r + k, D)}, device_id_type=MESH)

    hidden = ((sh_ref, zs, gs), (th_ref, zt, gt))
    for src, z, _ in hidden:
        x = src[...].astype(f32)
        half = z.shape[-1]
        for d in range(D):
            lo = x[:, 2 * d * half:(2 * d + 1) * half]
            hi = x[:, (2 * d + 1) * half:(2 * d + 2) * half]
            z[d] = jnp.concatenate([lo, hi], axis=0).astype(bf16)
    pl.semaphore_wait(barrier, F - 1 + D - 1)

    def z_copy(m, k):
        to = lax.rem(r + k, D)
        return remote(hidden[m][1].at[to], hidden[m][2].at[f, r], z_send.at[m, k], z_recv.at[m, k], dp=to)

    def z_in(m, k):
        return remote(hidden[m][1].at[0], hidden[m][2].at[f, lax.rem(r + D - k, D)], z_send.at[m, k], z_recv.at[m, k], dp=r)

    for m in range(2):
        for k in range(1, D):
            z_copy(m, k).start()
        hidden[m][2][f, r] = hidden[m][1][r]

    own = upper * H
    for b in range(nblk):
        a = act_ref[:, pl.ds(pl.multiple_of(own + b * LANES, LANES), LANES)].astype(f32)
        acol[b * LANES:(b + 1) * LANES, :] = jnp.broadcast_to(a, (LANES, LANES)).T

    def ag_copy(m, k):
        g = hidden[m][2]
        return remote(g.at[f], g.at[f], ag_send.at[m, k], ag_recv.at[m, k], fsdp=lax.rem(j + k, J) * 2 + core)

    def ag_slot(k):
        return lax.rem(j + J - k, J) * 2

    def pr_copy(m, k):
        g = hidden[m][2]
        s = ag_slot(k) + core
        return remote(g.at[s], g.at[s], pr_send.at[m, k], pr_recv.at[m, k], fsdp=partner)

    def pr_in(m, k):
        g = hidden[m][2]
        s = ag_slot(k) + 1 - core
        return remote(g.at[s], g.at[s], pr_send.at[m, k], pr_recv.at[m, k], fsdp=partner)

    for m in range(2):
        for k in range(1, D):
            z_in(m, k).wait_recv()
        for k in range(1, J):
            ag_copy(m, k).start()
        pr_copy(m, 0).start()

    def gather(m, rows):
        g = hidden[m][2]
        for k in range(1, J):
            s = ag_slot(k) + core
            remote(g.at[s], g.at[s], ag_send.at[m, k], ag_recv.at[m, k], fsdp=partner).wait_recv()
            pr_copy(m, k).start()
        for k in range(J):
            pr_in(m, k).wait_recv()
        half = g.shape[-1]
        n = g.shape[1] * 8

        @pl.loop(0, F)
        def _(b):
            x = g[b].astype(f32)
            at = pl.ds(pl.multiple_of(b * n, n), n)
            rows[at, :half] = x[:, 0:8, :].reshape(n, half).astype(bf16)
            rows[at, half:] = x[:, 8:16, :].reshape(n, half).astype(bf16)

    tile = max(LANES, min(V, 2**18 // T))

    def project(rows, w, m):
        @pl.loop(0, V // tile)
        def _(c):
            at = pl.ds(pl.multiple_of(c * tile, tile), tile)
            part[m, :, at] = jnp.dot(rows[...], w[:, at], preferred_element_type=f32)

    def line_copy(flow, i):
        to = jnp.clip(r + 1 - 2 * flow, 0, D - 1)
        return remote(line.at[flow, i], line.at[flow, i], l_send.at[flow, i], l_recv.at[flow, i], dp=to)

    near, far = upper, 1 - upper

    def own_rows(flow, i):
        return pl.ds(pl.multiple_of((1 - flow) * H + i * PIECE, PIECE), PIECE)

    def begin(m):
        @pl.when(end)
        def _():
            @pl.loop(0, NG)
            def _(i):
                encode(part[m, own_rows(near, i), :], line.at[near, m * NG + i])
                line_copy(near, m * NG + i).start()

    def pass_on(flow, p):
        line_copy(flow, p).wait_recv()
        x = part[p // NG, own_rows(flow, lax.rem(p, NG)), :] + decode(line.at[flow, p], V)
        encode(x, line.at[flow, p])
        line_copy(flow, p).start()

    def relay(first, last):
        @pl.when(jnp.logical_not(end))
        def _():
            @pl.loop(first, last)
            def _(p):
                @pl.when(p < 2 * NG)
                def _():
                    pass_on(near, p)

                @pl.when(p >= LAG)
                def _():
                    pass_on(far, p - LAG)

    def finish(m, i):
        line_copy(far, m * NG + i).wait_recv()
        at = own_rows(far, i)
        x = part[m, at, :] + decode(line.at[far, m * NG + i], V)
        part[m, at, :] = x
        return x

    gather(0, rows_s)
    w_s.wait()
    project(rows_s, ws, 0)
    begin(0)
    gather(1, rows_t)
    relay(0, NG // 2)
    w_t.wait()
    project(rows_t, wt, 1)
    begin(1)
    relay(NG // 2, 2 * NG + LAG)

    rows_x = wt.at[:ws.shape[0], :T]

    @pl.loop(0, T // LANES)
    def _(b):
        at = pl.ds(pl.multiple_of(b * LANES, LANES), LANES)
        rows_x[:, at] = rows_s[at, :].astype(f32).T.astype(bf16)

    rows_save = pltpu.make_async_copy(rows_x, rows_out, out_sem.at[0])
    rows_save.start()

    def st_copy(c, k):
        return remote(stats.at[c, f], stats.at[c, f], st_send.at[c, k], st_recv.at[c, k], fsdp=lax.rem(f + k, F))

    def st_in(c, k):
        s = lax.rem(f + F - k, F)
        return remote(stats.at[c, s], stats.at[c, s], st_send.at[c, k], st_recv.at[c, k], fsdp=s)

    def g_copy(half, i):
        at = pl.ds(pl.multiple_of(half * H + i * GPIECE, GPIECE), GPIECE)
        to = jnp.clip(r + 1 - 2 * half, 0, D - 1)
        return remote(grads.at[at], grads.at[at], g_send.at[half, i], g_recv.at[half, i], dp=to)

    def loss_copy(k):
        return remote(lossbuf, lossbuf, ls_send.at[k], ls_recv.at[0], dp=r + step * k)

    lane = lax.broadcasted_iota(i32, (PIECE, LANES), 1)
    column = lax.broadcasted_iota(i32, (PIECE, V), 1) + f * V

    @pl.when(end)
    def _():
        xcol[...] = jnp.zeros_like(xcol)

        @pl.loop(0, NG)
        def _(i):
            finish(0, i)

        def finish_chunk(c):
            block = pl.ds(c * CHUNK // LANES * LANES, LANES)
            first, last = c * CHUNK // PIECE, (c + 1) * CHUNK // PIECE

            @pl.loop(first, last)
            def _(i):
                here = pl.ds(pl.multiple_of(i * PIECE, PIECE), PIECE)
                lt = finish(1, i)
                ls = part[0, own_rows(far, i), :]
                mt, ms = jnp.max(lt, axis=1, keepdims=True), jnp.max(ls, axis=1, keepdims=True)
                et = jnp.exp(lt - mt)
                hit = column == acol[here, 0:1].astype(i32)
                values = (
                    mt, ms, jnp.sum(et, axis=1, keepdims=True), jnp.sum(jnp.exp(ls - ms), axis=1, keepdims=True),
                    jnp.sum(et * (lt - ls), axis=1, keepdims=True),
                    jnp.sum(jnp.where(hit, ls, 0.0), axis=1, keepdims=True))
                x = jnp.zeros((PIECE, LANES), f32)
                for n, v in enumerate(values):
                    x = jnp.where(lane == n, v, x)
                xcol[here, :] = x

            stats[c, f] = xcol[block, :].T[0:8, :]
            for k in range(1, F):
                st_copy(c, k).start()
            for k in range(1, F):
                st_in(c, k).wait_recv()
            s = stats[c]
            mt, ms = s[:, 0:1, :], s[:, 1:2, :]
            top_t, top_s = jnp.max(mt, axis=0), jnp.max(ms, axis=0)
            scale_t = jnp.exp(mt - top_t[None])
            sum_t = jnp.sum(s[:, 2:3, :] * scale_t, axis=0)
            sum_s = jnp.sum(s[:, 3:4, :] * jnp.exp(ms - top_s[None]), axis=0)
            cross = jnp.sum(s[:, 4:5, :] * scale_t, axis=0)
            pick = jnp.sum(s[:, 5:6, :], axis=0)
            lse_t, lse_s = top_t + jnp.log(sum_t), top_s + jnp.log(sum_s)
            at = pl.ds(pl.multiple_of(own + c * CHUNK // LANES * LANES, LANES), LANES)
            weight, benefit = mask_ref[:, at].astype(f32), adv_ref[:, at]
            kl = cross / sum_t - lse_t + lse_s
            loss = weight * (KL_WEIGHT * kl - benefit * (pick - lse_s))
            lossbuf[c * 8:(c + 1) * 8, :] = jnp.broadcast_to(loss, (8, LANES))
            y = jnp.concatenate(
                [jnp.broadcast_to(v, (8, LANES)) for v in (lse_t, lse_s, weight, benefit)]
                + [jnp.zeros((LANES - 32, LANES), f32)], axis=0)
            skip = c * CHUNK % LANES
            ycol[c * CHUNK:(c + 1) * CHUNK, :] = y.T[skip:skip + CHUNK, :]

            @pl.loop(first, last)
            def _(i):
                at = own_rows(far, i)
                here = pl.ds(pl.multiple_of(i * PIECE, PIECE), PIECE)
                lse_t, lse_s = ycol[here, 0:1], ycol[here, 8:9]
                weight, benefit = ycol[here, 16:17], ycol[here, 24:25]
                tp, sp = jnp.exp(part[1, at, :] - lse_t), jnp.exp(part[0, at, :] - lse_s)
                hit = (column == acol[here, 0:1].astype(i32)).astype(f32)
                g = weight * (KL_WEIGHT * (sp - tp) + benefit * (sp - hit))
                grads[at, :] = g.astype(bf16)
                for n in range(PIECE // GPIECE):
                    g_copy(upper, i * (PIECE // GPIECE) + n).start()

        for c in range(NC):
            finish_chunk(c)

        for k in range(1, D // 2):
            loss_copy(k).start()

    feature = ws.shape[0]
    ftile = min(512, feature)

    def back(half):
        at = pl.ds(pl.multiple_of(half * H, H), H)

        @pl.loop(0, feature // ftile)
        def _(c):
            cols = pl.ds(pl.multiple_of(c * ftile, ftile), ftile)
            y = lax.dot_general(grads[at, :], ws[cols, :], (((1,), (1,)), ((), ())), preferred_element_type=f32)
            part[0, at, cols] = y

    def hg(b, c):
        at = pl.ds(pl.multiple_of((b * 2 + c) * TB, TB), TB)
        return part.at[0, at, :feature]

    def pair_copy(b):
        return remote(hg(b, 1 - core), pair_in.at[b], hp_send.at[b], hp_recv.at[b], fsdp=partner)

    def hd_copy(b):
        return remote(hg(b, core), peer_in.at[j], hd_send.at[b], hd_recv.at[j], fsdp=b * 2 + core)

    def hd_in(b):
        return remote(hg(b, core), peer_in.at[b], hd_send.at[b], hd_recv.at[b], fsdp=f)

    def pair_start(half):
        @pl.loop(0, J // 2)
        def _(n):
            pair_copy(half * (J // 2) + n).start()

    def share_out(half):
        @pl.loop(0, J // 2)
        def _(n):
            b = half * (J // 2) + n
            pair_copy(b).wait()
            y = hg(b, core)[...] + pair_in[b]

            @pl.when(b == j)
            def _():
                peer_in[j] = y

            @pl.when(b != j)
            def _():
                hg(b, core)[...] = y
                hd_copy(b).start()

    @pl.when(jnp.logical_not(end))
    def _():
        @pl.loop(0, GG + GLAG)
        def _(i):
            @pl.when(i < GG)
            def _():
                g_copy(upper, i).wait_recv()
                g_copy(upper, i).start()

            @pl.when(i >= GLAG)
            def _():
                g_copy(1 - upper, i - GLAG).wait_recv()
                g_copy(1 - upper, i - GLAG).start()

    back(upper)
    pair_start(upper)
    share_out(upper)

    @pl.when(end)
    def _():
        @pl.loop(0, GG)
        def _(i):
            g_copy(1 - upper, i).wait_recv()

    grad_save = pltpu.make_async_copy(grads, grad_out, out_sem.at[1])
    grad_save.start()
    back(1 - upper)
    pair_start(1 - upper)
    share_out(1 - upper)

    @pl.when(jnp.logical_not(end))
    def _():
        loss_copy(0).wait_recv()
    losses = jnp.concatenate(
        [lossbuf[c * 8:c * 8 + 1, c * CHUNK % LANES:c * CHUNK % LANES + CHUNK] for c in range(NC)], axis=1)
    share = T // D
    for q in range(D // 2):
        @pl.when(lax.rem(r, D // 2) == q)
        def _():
            loss_ref[...] = losses[:, q * share:(q + 1) * share]

    for k in range(1, J):
        hd_in(lax.rem(j + k, J)).wait_recv()
    hid_ref[...] = jnp.sum(peer_in[...], axis=0).astype(bf16)

    for m in range(2):
        for k in range(1, D):
            z_copy(m, k).wait_send()
        for k in range(1, J):
            ag_copy(m, k).wait_send()
        for k in range(J):
            pr_copy(m, k).wait_send()
    for k in range(1, J):
        hd_copy(lax.rem(j + k, J)).wait_send()

    @pl.loop(0, 2 * NG)
    def _(i):
        line_copy(near, i).wait_send()

    @pl.loop(0, GG)
    def _(i):
        g_copy(upper, i).wait_send()

    @pl.when(end)
    def _():
        for k in range(1, F):
            for c in range(NC):
                st_copy(c, k).wait_send()
        for k in range(1, D // 2):
            loss_copy(k).wait_send()

    @pl.when(jnp.logical_not(end))
    def _():
        @pl.loop(0, 2 * NG)
        def _(i):
            line_copy(far, i).wait_send()

        @pl.loop(0, GG)
        def _(i):
            g_copy(1 - upper, i).wait_send()

    rows_save.wait()
    grad_save.wait()


def head_grad_kernel(rows_ref, grad_ref, out_ref):
    out_ref[...] = jnp.dot(rows_ref[...], grad_ref[...], preferred_element_type=f32)


def shards(F, D, teacher_hidden, student_hidden, teacher_head, student_head, actions, advantages, loss_mask):
    T = actions.shape[0]
    kt, V = teacher_head.shape
    ks = student_head.shape[0]
    mine = teacher_hidden.shape[0]
    J, H, TB = F // 2, T // 2, T // F
    NG, GG, NC = H // PIECE, H // GPIECE, H // CHUNK
    vmem = pl.BlockSpec(memory_space=pltpu.VMEM)
    hbm = pl.BlockSpec(memory_space=pl.ANY)
    dma = pltpu.SemaphoreType.DMA
    loss, hidden_grad, rows, grads = pl.pallas_call(
        functools.partial(main_kernel, F, D),
        out_shape=(
            jax.ShapeDtypeStruct((1, T // D), f32),
            jax.ShapeDtypeStruct((TB, ks), bf16),
            jax.ShapeDtypeStruct((ks, T), bf16),
            jax.ShapeDtypeStruct((T, V), bf16),
        ),
        in_specs=[vmem, vmem, hbm, hbm, vmem, vmem, vmem],
        out_specs=(vmem, vmem, hbm, hbm),
        scratch_shapes=[
            pltpu.VMEM((kt, V), bf16),
            pltpu.VMEM((ks, V), bf16),
            pltpu.VMEM((D, 2 * mine, kt // 2), bf16),
            pltpu.VMEM((D, 2 * mine, ks // 2), bf16),
            pltpu.VMEM((F, D, 2 * mine, kt // 2), bf16),
            pltpu.VMEM((F, D, 2 * mine, ks // 2), bf16),
            pltpu.VMEM((T, kt), bf16),
            pltpu.VMEM((T, ks), bf16),
            pltpu.VMEM((2, T, V), f32),
            pltpu.VMEM((2, 2 * NG, PIECE, V + LANES), i16),
            pltpu.VMEM((H, LANES), f32),
            pltpu.VMEM((NC, F, 8, LANES), f32),
            pltpu.VMEM((H, LANES), f32),
            pltpu.VMEM((H, LANES), f32),
            pltpu.VMEM((NC * 8, LANES), f32),
            pltpu.VMEM((T, V), bf16),
            pltpu.VMEM((J, TB, ks), f32),
            pltpu.VMEM((J, TB, ks), f32),
            dma((2,)),
            dma((2, D)), dma((2, D)),
            dma((2, J)), dma((2, J)),
            dma((2, J)), dma((2, J)),
            dma((2, 2 * NG)), dma((2, 2 * NG)),
            dma((NC, F)), dma((NC, F)),
            dma((2, GG)), dma((2, GG)),
            dma((J,)), dma((J,)),
            dma((J,)), dma((J,)),
            dma((D,)), dma((1,)),
            dma((2,)),
        ],
        compiler_params=pltpu.CompilerParams(
            collective_id=0, has_side_effects=True, vmem_limit_bytes=63 * 2**20),
    )(teacher_hidden, student_hidden, teacher_head, student_head,
      actions.reshape(1, T), advantages.reshape(1, T), loss_mask.reshape(1, T))
    tile = min(256, ks)
    head_grad = pl.pallas_call(
        head_grad_kernel,
        grid=(ks // tile,),
        out_shape=jax.ShapeDtypeStruct((ks, V), f32),
        in_specs=[pl.BlockSpec((tile, T), lambda c: (c, 0)), pl.BlockSpec((T, V), lambda c: (0, 0))],
        out_specs=pl.BlockSpec((tile, V), lambda c: (c, 0)),
        compiler_params=pltpu.CompilerParams(vmem_limit_bytes=63 * 2**20),
    )(rows, grads)
    return loss.reshape(T // D), head_grad, hidden_grad


def solution(mesh):
    placed = (
        P(("fsdp", "dp"), None),
        P(("fsdp", "dp"), None),
        P("dp", "fsdp"),
        P("dp", "fsdp"),
        P(),
        P(),
        P(),
    )
    return jax.shard_map(
        functools.partial(shards, mesh.shape["fsdp"], mesh.shape["dp"]),
        mesh=mesh,
        in_specs=placed,
        out_specs=(P("dp"), P("dp", "fsdp"), P("fsdp", "dp")),
        check_vma=False,
    )
```
